256 devices in a mesh: section: 16 (over x_lo, y, core), dp: 16 (over z, x_hi).
Axes of the slice: x: 4 (x_hi: 2, x_lo: 2; x = x_hi * 2 + x_lo), y: 4, z: 8, core: 2. Of those that a mesh axis runs over, the one named last changes fastest.
Arguments:
- activations: bfloat16 [16, 16, 64, 4096], P('section', 'dp'), may hold values from -6 to 6
- cotangents: bfloat16 [16, 16, 64, 14336], P('section', 'dp'), may hold values from -6 to 6
- mb_count: int32 [16, 16], P('section', 'dp'), may hold values from 2 to 4, as said below
- mb_size: int32 [16, 16, 4], P('section', 'dp'), may hold values from 8 to 16, as said below
- block_slot: int32 [16, 32], P('section'), may hold values from 0 to 31, as said below
- inv_blocks: bfloat16 [16, 32, 512, 512], P('section', 'dp'), may hold values from -1.5 to 1.5
Outputs:
- preconditioned: bfloat16 [16, 32, 512, 2048], P('section', 'dp')
- output_stats: bfloat16 [16, 32, 512, 256], P('section', 'dp')
- input_stats: float32 [16, 2048, 512], P('section', 'dp')
The draws below stay inside these ranges and needn't reach their ends.
Inputs may be any that keep to these rules, and one draw needn't show every extreme that they name: `mb_count`: A device's live microbatches are its first slots; some device uses all 4. `mb_size`: some slot of some device is full. `block_slot`: on each section the first 28 entries are the slots of the hidden blocks and the next 4 those of the input blocks of the section's half; all distinct; slot q lies on dp device q // 2; the last slot is always taken.
All inputs are finite; a program needn't handle non-finite values.
Results may differ from the reference program's by a relative error of at most 0.015.
Values may be sent and summed in bfloat16 or wider, within the bound.
No kernel may reach another device: no remote copies, remote signals or barrier semaphores. Data moves between devices by JAX's collectives and lax.ppermute only.
A program may use at most 128 MiB of HBM per device.

```python
import jax
import jax.numpy as jnp

DW = 4096
FW = 14336
BLK = 512
TOK_DEV = 64
MB = 4
NG = 28
ABH = 4
TSLOT = 2
N_SECTION = 16
N_DP = 16


def draw_mb_count(key, part):
    key = jax.random.fold_in(key, 11)
    first_key, second_key = jax.random.split(key)
    counts = jax.random.randint(first_key, (N_SECTION, N_DP), MB // 2, MB + 1)
    position = jax.random.randint(second_key, (), 0, N_SECTION * N_DP)
    flattened = counts.reshape(-1).at[position].set(MB)
    return flattened.reshape(N_SECTION, N_DP).astype(jnp.int32)


def draw_mb_size(key, part):
    key = jax.random.fold_in(key, 23)
    first_key, second_key = jax.random.split(key)
    per_slot = TOK_DEV // MB
    sizes = jax.random.randint(first_key, (N_SECTION * N_DP * MB,), per_slot // 2, per_slot + 1)
    position = jax.random.randint(second_key, (), 0, N_SECTION * N_DP * MB)
    sizes = sizes.at[position].set(per_slot)
    return sizes.reshape(N_SECTION, N_DP, MB).astype(jnp.int32)


def draw_block_slot(key, part):
    key = jax.random.fold_in(key, 37)
    slot_total = N_DP * TSLOT
    block_total = NG + ABH
    section_keys = jax.random.split(key, N_SECTION)
    permuted = jax.vmap(lambda section_key: jax.random.permutation(section_key, slot_total))(section_keys)[:, :block_total]
    present = jnp.any(permuted == slot_total - 1, axis=1)
    leading = jnp.where(present, permuted[:, 0], slot_total - 1)
    permuted = permuted.at[:, 0].set(leading)
    return permuted.astype(jnp.int32)


def level_of(stream_key, dims, shards, low, high):
    def one(dim, blocks):
        draws = jax.random.uniform(jax.random.fold_in(jax.random.fold_in(stream_key, 6), dim), (blocks,), jnp.float32, low / len(shards), high / len(shards))
        return jnp.repeat(jnp.exp(draws), dims[dim] // blocks).reshape((-1,) + (1,) * (len(dims) - dim - 1))

    loudness = one(*shards[0])
    for cut in shards[1:]:
        loudness = loudness * one(*cut)
    return loudness


def normal_values(stream_key, shape, scale, bound, cuts=(), held_as=jnp.bfloat16):
    factor_of = level_of(stream_key, shape, cuts, -0.22, 0.18) if cuts else 1.0
    values = jax.random.normal(stream_key, shape, jnp.float32) * scale * factor_of
    return jnp.minimum(jnp.maximum(values, -bound), bound).astype(held_as)


def setup_inputs(seed: int = 0) -> dict:
    key_of = jax.random.split(jax.random.key(seed), 7)
    return {
        "activations": normal_values(key_of[0], (N_SECTION, N_DP, TOK_DEV, DW), 1.0, 6.0, ((0, 16), (1, 16))),
        "cotangents": normal_values(key_of[1], (N_SECTION, N_DP, TOK_DEV, FW), 1.0, 6.0, ((0, 16), (1, 16))),
        "mb_count": draw_mb_count(jax.random.fold_in(key_of[6], 71), 0),
        "mb_size": draw_mb_size(jax.random.fold_in(key_of[6], 71), 0),
        "block_slot": draw_block_slot(jax.random.fold_in(key_of[6], 71), 0),
        "inv_blocks": normal_values(key_of[5], (N_SECTION, N_DP * TSLOT, BLK, BLK), 0.25, 1.5, ((0, 16), (1, 16))),
    }


def live_mask(count_live, sizes, rows_total, per_slot):
    index = jnp.arange(rows_total, dtype=jnp.int32)
    group = index // per_slot
    within = index % per_slot
    slot_ids = jnp.arange(sizes.shape[0], dtype=jnp.int32)
    picked = jnp.sum(jnp.where(group[:, None] == slot_ids[None, :], sizes[None, :], 0), axis=1)
    return (group < count_live) & (within < picked)


def reference(activations, cotangents, mb_count, mb_size, block_slot, inv_blocks):
    per_slot = TOK_DEV // MB
    half_width = DW // 2
    half_block = BLK // 2
    slot_total = N_DP * TSLOT
    masker = jax.vmap(jax.vmap(lambda count_live, sizes: live_mask(count_live, sizes, TOK_DEV, per_slot)))
    live_rows = masker(mb_count, mb_size)
    zero_bf = jnp.zeros((), jnp.bfloat16)
    masked_x = jnp.where(live_rows[..., None], activations, zero_bf)
    masked_g = jnp.where(live_rows[..., None], cotangents, zero_bf)
    live_counts = jnp.sum(live_rows.astype(jnp.int32), axis=2)
    precond_list = []
    output_list = []
    input_list = []
    for section_id in range(N_SECTION):
        mirror_id = N_SECTION - 1 - section_id
        half_index = 1 if section_id >= N_SECTION // 2 else 0
        token_total = (jnp.sum(live_counts[section_id]) + jnp.sum(live_counts[mirror_id])).astype(jnp.float32)
        x_rows = jnp.concatenate([masked_x[section_id], masked_x[mirror_id]], axis=0).reshape(-1, DW)
        x_rows = x_rows[:, half_index * half_width:(half_index + 1) * half_width]
        g_rows = jnp.concatenate([masked_g[section_id], masked_g[mirror_id]], axis=0).reshape(-1, FW)
        grad_mean = jnp.dot(g_rows.T, x_rows, preferred_element_type=jnp.float32) / token_total
        x_blocks = x_rows.reshape(-1, ABH, BLK).astype(jnp.float32)
        in_stat = jnp.einsum('rki,rkj->kij', x_blocks, x_blocks).reshape(half_width, BLK) / token_total
        g_blocks = g_rows.reshape(-1, NG, BLK).astype(jnp.float32)
        g_half = g_blocks[:, :, half_index * half_block:(half_index + 1) * half_block]
        out_stat = jnp.einsum('rbi,rbj->bij', g_blocks, g_half) / token_total
        slot_table = block_slot[section_id]
        hidden_table = slot_table[:NG]
        input_table = slot_table[NG:]
        slot_index = jnp.arange(slot_total, dtype=jnp.int32)
        matches = hidden_table[None, :] == slot_index[:, None]
        used = jnp.any(matches, axis=1)
        which = jnp.sum(jnp.where(matches, jnp.arange(NG, dtype=jnp.int32)[None, :], 0), axis=1).astype(jnp.int32)
        grad_slot = jnp.where(used[:, None, None], jnp.take(grad_mean.reshape(NG, BLK, half_width), which, axis=0), 0.0).astype(jnp.bfloat16)
        stat_slot = jnp.where(used[:, None, None], jnp.take(out_stat, which, axis=0), 0.0).astype(jnp.bfloat16)
        a_inverse = jnp.take(inv_blocks[section_id], input_table, axis=0)
        left = jnp.einsum('qij,qjc->qic', inv_blocks[section_id].astype(jnp.float32), grad_slot.astype(jnp.float32)).astype(jnp.bfloat16)
        left = left.reshape(slot_total, BLK, ABH, BLK).astype(jnp.float32)
        scaled = jnp.einsum('qikj,kjc->qikc', left, a_inverse.astype(jnp.float32)).astype(jnp.bfloat16)
        scaled = scaled.reshape(slot_total, BLK, half_width)
        scaled = jnp.where(used[:, None, None], scaled, jnp.zeros((), jnp.bfloat16))
        precond_list.append(scaled)
        output_list.append(stat_slot)
        input_list.append(in_stat.astype(jnp.float32))
    return (jnp.stack(precond_list), jnp.stack(output_list), jnp.stack(input_list))
```

```python
import functools

import jax
import jax.numpy as jnp
from jax import lax
from jax.experimental import pallas as pl
from jax.experimental.pallas import tpu as pltpu
from jax.sharding import PartitionSpec as P

MB = 4
VMEM_BYTES = 56 * 1024 * 1024


def z_step(value, step):
    count = lax.axis_size("dp")
    pairs = [(d, (d + 2 * step) % count) for d in range(count)]
    return lax.ppermute(value, "dp", pairs)


def x_swap(value):
    count = lax.axis_size("dp")
    return lax.ppermute(value, "dp", [(d, d ^ 1) for d in range(count)])


def ring_start(start):
    return z_step(start, 1), z_step(start, -1)


def ring_start_pair(up, down):
    return z_step(up, 1), z_step(down, -1)


def ring_end(up, down):
    cut = up.shape[0] // 2
    return z_step(up[:cut], 1), z_step(down[cut:], -1)


def live_mask(count_live, sizes, rows_total, per_slot):
    index = jnp.arange(rows_total, dtype=jnp.int32)
    group = index // per_slot
    within = index % per_slot
    slot_ids = jnp.arange(sizes.shape[0], dtype=jnp.int32)
    picked = jnp.sum(jnp.where(group[:, None] == slot_ids[None, :], sizes[None, :], 0), axis=1)
    return (group < count_live) & (within < picked)


def contract_rows(first_mat, second_mat):
    return lax.dot_general(
        first_mat, second_mat, (((0,), (0,)), ((), ())), preferred_element_type=jnp.float32
    )


def route_kernel(slots_here, pick, limit, g_ref, out_ref):
    rows, _ = g_ref.shape
    dests, _, block = out_ref.shape
    per = rows // MB
    within = lax.broadcasted_iota(jnp.int32, (per, block), 0)
    keep = [within < limit[m] for m in range(MB)]

    @pl.loop(0, dests)
    def _(dest):
        for t in range(slots_here):
            number = pick[dest * slots_here + t]
            start = pl.multiple_of(number * block, block)
            for m in range(MB):
                part = g_ref[pl.ds(m * per, per), pl.ds(start, block)]
                part = jnp.where(keep[m], part, jnp.zeros_like(part))
                out_ref[dest, pl.ds(t * rows + m * per, per), :] = part


def route(pick, limit, g_rows, dests, slots_here, block):
    vmem = pl.BlockSpec(memory_space=pltpu.VMEM)
    smem = pl.BlockSpec(memory_space=pltpu.SMEM)
    return pl.pallas_call(
        functools.partial(route_kernel, slots_here),
        out_shape=jax.ShapeDtypeStruct((dests, slots_here * g_rows.shape[0], block), jnp.bfloat16),
        in_specs=[smem, smem, vmem],
        out_specs=vmem,
        compiler_params=pltpu.CompilerParams(vmem_limit_bytes=VMEM_BYTES),
        cost_estimate=pl.CostEstimate(flops=0, bytes_accessed=8 * 2**20, transcendentals=0),
    )(pick, limit, g_rows)


def pack_routed(rows, source, routed_ref, packed, turned):
    for t in range(turned.shape[0]):
        for n in range(routed_ref.shape[0]):
            packed[t, pl.ds(n * rows, rows), :] = routed_ref[source[n], pl.ds(t * rows, rows), :]
        turned[t] = packed[t].T


def half_columns(packed, t, half, half_block):
    return packed[t, :, pl.ds(pl.multiple_of(half * half_block, half_block), half_block)]


def gram_here(place, xs, width):
    cols = xs[:, pl.ds(pl.multiple_of(place[3] * width, width), width)]
    return jnp.dot(cols.T, xs[...], preferred_element_type=jnp.float32)


def ring_rows(shards, first, count):
    picked = []
    for d in range(4):
        picked.append([(shards[d], first, count)])
    top, bottom = shards[4], shards[5]
    cut = top.shape[0]
    upper = min(max(cut - first, 0), count)
    parts = []
    if upper:
        parts.append((top, first, upper))
    if upper < count:
        parts.append((bottom, first + upper - cut, count - upper))
    picked.append(parts)
    for d in (6, 7, 8):
        picked.append([(shards[d], first, count)])
    return picked


def first_kernel(rows, held, source, place, routed_ref, *refs):
    shards, (acc_ref, stat_ref, gram_ref, packed, turned, xs) = refs[:9], refs[9:]
    k = pl.program_id(0)

    @pl.when(k == 0)
    def _():
        pack_routed(rows, source, routed_ref, packed, turned)
        for t in range(turned.shape[0]):
            cols = half_columns(packed, t, place[0], stat_ref.shape[2])
            stat_ref[t] = jnp.dot(turned[t], cols, preferred_element_type=jnp.float32)

    at = 0
    mine, other = ring_rows(shards, 0, rows), ring_rows(shards, held, rows)
    for d in range(8):
        for ref, start, count in mine[d] + other[d]:
            xs[pl.ds(at, count), :] = ref[pl.ds(start, count), :]
            at += count
    for t in range(turned.shape[0]):
        acc_ref[t] = jnp.dot(turned[t], xs[...], preferred_element_type=jnp.float32)

    @pl.when(k == place[2])
    def _():
        gram_ref[...] = gram_here(place, xs, gram_ref.shape[0])


def column_spec(array, block):
    return pl.BlockSpec((array.shape[0], block), lambda k: (0, k))


def first_part(source, place, routed, shards, rows, held, slots_here, block):
    width = shards[0].shape[1]
    tokens = routed.shape[0] * rows
    gram_rows = width // routed.shape[0]
    vmem = pl.BlockSpec(memory_space=pltpu.VMEM)
    smem = pl.BlockSpec(memory_space=pltpu.SMEM)
    flops = 2 * slots_here * block * tokens * (width + block // 2)
    return pl.pallas_call(
        functools.partial(first_kernel, rows, held),
        grid=(width // block,),
        out_shape=(
            jax.ShapeDtypeStruct((slots_here, block, width), jnp.float32),
            jax.ShapeDtypeStruct((slots_here, block, block // 2), jnp.float32),
            jax.ShapeDtypeStruct((gram_rows, block), jnp.float32),
        ),
        in_specs=[smem, smem, vmem] + [column_spec(s, block) for s in shards],
        out_specs=(
            pl.BlockSpec((slots_here, block, block), lambda k: (0, 0, k)),
            pl.BlockSpec((slots_here, block, block // 2), lambda k: (0, 0, 0)),
            pl.BlockSpec((gram_rows, block), lambda k: (0, 0)),
        ),
        scratch_shapes=[
            pltpu.VMEM((slots_here, tokens, block), jnp.bfloat16),
            pltpu.VMEM((slots_here, block, tokens), jnp.bfloat16),
            pltpu.VMEM((tokens, block), jnp.bfloat16),
        ],
        compiler_params=pltpu.CompilerParams(vmem_limit_bytes=VMEM_BYTES),
        cost_estimate=pl.CostEstimate(flops=flops, bytes_accessed=16 * 2**20, transcendentals=0),
    )(source, place, routed, *shards)


def last_kernel(rows, first_late, source, place, used, scale, routed_ref, *refs):
    shards, swapped = refs[:9], refs[9:13]
    acc_ref, stat1_ref, gram1_ref, inv_ref, a_ref, out_ref, stat_ref, gram_ref, packed, turned, xs = refs[13:]
    k = pl.program_id(0)
    per_token = scale[0]

    @pl.when(k == 0)
    def _():
        pack_routed(rows, source, routed_ref, packed, turned)
        for t in range(turned.shape[0]):
            cols = half_columns(packed, t, place[0], stat_ref.shape[2])
            stat = stat1_ref[t] + jnp.dot(turned[t], cols, preferred_element_type=jnp.float32)
            stat_ref[t] = jnp.where(used[t] > 0, stat * per_token, 0.0).astype(stat_ref.dtype)

    one, two, three, four = swapped
    late = four.shape[0]
    partner = [(one, 0), (one, 1), (two, 0), (three, 0), (four, 0), (three, 1), (two, 1), (one, 2)]
    mine = ring_rows(shards, first_late, rows)
    at = 0
    for d in range(8):
        ref, number = partner[d]
        for ref, start, count in mine[d] + [(ref, number * late, rows)]:
            xs[pl.ds(at, count), :] = ref[pl.ds(start, count), :]
            at += count

    for t in range(turned.shape[0]):
        grad = acc_ref[t] + jnp.dot(turned[t], xs[...], preferred_element_type=jnp.float32)
        grad = (grad * per_token).astype(jnp.bfloat16)
        left = jnp.dot(inv_ref[t], grad, preferred_element_type=jnp.float32).astype(jnp.bfloat16)
        scaled = jnp.dot(left, a_ref[0], preferred_element_type=jnp.float32)
        out_ref[t] = jnp.where(used[t] > 0, scaled, 0.0).astype(out_ref.dtype)

    @pl.when(k == place[2])
    def _():
        gram_ref[...] = (gram1_ref[...] + gram_here(place, xs, gram_ref.shape[0])) * per_token


def last_part(source, place, used, scale, routed, shards, swapped, acc, stat1, gram1, inverses, a_inverse, rows, first_late):
    width = acc.shape[2]
    slots_here, block = inverses.shape[:2]
    tokens = routed.shape[0] * rows
    vmem = pl.BlockSpec(memory_space=pltpu.VMEM)
    smem = pl.BlockSpec(memory_space=pltpu.SMEM)
    flops = 2 * slots_here * block * width * (tokens + 2 * block)
    return pl.pallas_call(
        functools.partial(last_kernel, rows, first_late),
        grid=(width // block,),
        out_shape=(
            jax.ShapeDtypeStruct((slots_here, block, width), jnp.bfloat16),
            jax.ShapeDtypeStruct((slots_here, block, block // 2), jnp.bfloat16),
            jax.ShapeDtypeStruct(gram1.shape, jnp.float32),
        ),
        in_specs=[smem, smem, smem, smem, vmem]
        + [column_spec(s, block) for s in list(shards) + list(swapped)]
        + [
            pl.BlockSpec((slots_here, block, block), lambda k: (0, 0, k)), vmem, vmem, vmem,
            pl.BlockSpec((1, block, block), lambda k: (k, 0, 0)),
        ],
        out_specs=(
            pl.BlockSpec((slots_here, block, block), lambda k: (0, 0, k)),
            pl.BlockSpec((slots_here, block, block // 2), lambda k: (0, 0, 0)),
            pl.BlockSpec(gram1.shape, lambda k: (0, 0)),
        ),
        scratch_shapes=[
            pltpu.VMEM((slots_here, tokens, block), jnp.bfloat16),
            pltpu.VMEM((slots_here, block, tokens), jnp.bfloat16),
            pltpu.VMEM((tokens, block), jnp.bfloat16),
        ],
        compiler_params=pltpu.CompilerParams(vmem_limit_bytes=VMEM_BYTES),
        cost_estimate=pl.CostEstimate(flops=flops, bytes_accessed=24 * 2**20, transcendentals=0),
    )(source, place, used, scale, routed, *shards, *swapped, acc, stat1, gram1, inverses, a_inverse)


def local(activations, cotangents, mb_count, mb_size, block_slot, inv_blocks):
    rows = activations.shape[2]
    width = activations.shape[3]
    hidden_width = cotangents.shape[3]
    block = inv_blocks.shape[2]
    slots_here = inv_blocks.shape[1]
    half_width = width // 2
    hidden_blocks = hidden_width // block
    input_blocks = half_width // block
    section_count = lax.axis_size("section")
    dp_count = lax.axis_size("dp")
    section_id = lax.axis_index("section")
    dp_id = lax.axis_index("dp")
    half = (section_id >= section_count // 2).astype(jnp.int32)
    zero_bf = jnp.zeros((), jnp.bfloat16)
    mirror = [(s, section_count - 1 - s) for s in range(section_count)]

    x_all = activations[0, 0]
    g_raw = cotangents[0, 0]
    local_blocks = inv_blocks[0]
    meta = jnp.concatenate([mb_count[0], mb_size[0, 0]])
    meta_m = lax.ppermute(meta, "section", mirror)
    x_sent = lax.dynamic_slice_in_dim(x_all, (1 - half) * half_width, half_width, 1)
    x_m = lax.ppermute(x_sent, "section", mirror)
    g_m = lax.ppermute(g_raw, "section", mirror)

    def limits(numbers):
        return jnp.where(jnp.arange(MB, dtype=jnp.int32) < numbers[0], numbers[1:], 0)

    slot_table = block_slot[0]
    hidden_table = slot_table[:hidden_blocks]
    input_table = slot_table[hidden_blocks:]
    hidden_ids = jnp.arange(hidden_blocks, dtype=jnp.int32)
    every_slot = jnp.arange(dp_count * slots_here, dtype=jnp.int32)
    slot_matches = hidden_table[None, :] == every_slot[:, None]
    block_pick = jnp.sum(jnp.where(slot_matches, hidden_ids[None, :], 0), axis=1)
    my_slots = dp_id * slots_here + jnp.arange(slots_here, dtype=jnp.int32)
    used_here = jnp.any(hidden_table[None, :] == my_slots[:, None], axis=1).astype(jnp.int32)

    z_count = dp_count // 2
    z_here, x_here = dp_id // 2, lax.rem(dp_id, 2)

    out_own = route(block_pick, limits(meta), g_raw, dp_count, slots_here, block)

    live_own = live_mask(meta[0], meta[1:], rows, rows // MB)
    live_mir = live_mask(meta_m[0], meta_m[1:], rows, rows // MB)
    count = jnp.sum(live_own.astype(jnp.int32)) + jnp.sum(live_mir.astype(jnp.int32))
    x_own = lax.dynamic_slice_in_dim(x_all, half * half_width, half_width, 1)
    x_own = jnp.where(live_own[:, None], x_own, zero_bf)
    x_mir = jnp.where(live_mir[:, None], x_m, zero_bf)
    held = rows
    first_late = 2 * held
    start = jnp.concatenate([x_own, x_swap(x_own), x_mir], axis=0)

    half_block = block // 2
    piece = half_block // z_count
    kept = lax.dynamic_slice_in_dim(local_blocks, x_here * half_block, half_block, 1)
    given = lax.dynamic_slice_in_dim(local_blocks, (1 - x_here) * half_block, half_block, 1)
    near = jnp.concatenate([kept, x_swap(given)], axis=0)
    owner = input_table // slots_here
    near_index = jnp.where(owner % 2 == x_here, 0, slots_here) + input_table % slots_here
    part = jnp.where((owner // 2 == z_here)[:, None, None], jnp.take(near, near_index, axis=0), zero_bf)
    part = part.reshape(input_blocks, z_count, piece, block)

    def part_for(offset):
        return lax.dynamic_index_in_dim(part, lax.rem(z_here + offset + z_count, z_count), 1, keepdims=False)

    out_mir = route(block_pick, limits(meta_m), g_m, dp_count, slots_here, block)

    def late_swap(*parts):
        return x_swap(jnp.concatenate([part[first_late:] for part in parts], axis=0))

    up1, down1 = ring_start(start)
    sum_up, sum_down = z_step(part_for(4), 1), z_step(part_for(-3), -1)
    one = late_swap(start, up1, down1)
    up2, down2 = ring_start_pair(up1, down1)
    sum_up, sum_down = z_step(part_for(3) + sum_up, 1), z_step(part_for(-2) + sum_down, -1)
    two = late_swap(up2, down2)
    up3, down3 = ring_start_pair(up2, down2)
    sum_up, sum_down = z_step(part_for(2) + sum_up, 1), z_step(part_for(-1) + sum_down, -1)
    up3, down3, out_own = lax.optimization_barrier((up3, down3, out_own))
    in_own = lax.all_to_all(out_own, "dp", split_axis=0, concat_axis=0, tiled=True)
    three = late_swap(up3, down3)
    top4, bottom4 = ring_end(up3, down3)
    sum_up = z_step(part_for(1) + sum_up, 1)
    mine = (part_for(0) + sum_up + sum_down).reshape(input_blocks * piece, block)
    cut = top4.shape[0]
    opposite = jnp.concatenate([top4, bottom4], axis=0)[first_late:] if first_late < cut else bottom4[first_late - cut :]
    four = x_swap(opposite)
    shards = [start, up1, up2, up3, top4, bottom4, down3, down2, down1]

    in_mir = lax.all_to_all(out_mir, "dp", split_axis=0, concat_axis=0, tiled=True)

    counts = jnp.full((16, block), count.astype(jnp.bfloat16))
    a0 = jnp.concatenate([mine, counts], axis=0)
    a_up1, a_down1 = ring_start(a0)
    a_up2, a_down2 = ring_start_pair(a_up1, a_down1)
    a_up3, a_down3 = ring_start_pair(a_up2, a_down2)
    a_four = jnp.concatenate([z_step(a_up3[: a0.shape[0] // 2], 1), z_step(a_down3[a0.shape[0] // 2 :], -1)], axis=0)
    a_one = x_swap(jnp.concatenate([a0, a_up1, a_down1], axis=0)).reshape(3, -1, block)
    a_two = x_swap(jnp.concatenate([a_up2, a_down2], axis=0)).reshape(2, -1, block)
    a_three = x_swap(jnp.concatenate([a_up3, a_down3], axis=0)).reshape(2, -1, block)
    a_last = x_swap(a_four)
    near_parts = [a0, a_up1, a_up2, a_up3, a_four, a_down3, a_down2, a_down1]
    far_parts = [a_one[0], a_one[1], a_two[0], a_three[0], a_last, a_three[1], a_two[1], a_one[2]]

    z_from = lax.rem(z_here - jnp.arange(z_count, dtype=jnp.int32) + z_count, z_count)
    x_order = jnp.stack([x_here, 1 - x_here])
    source = (z_from[:, None] * 2 + x_order[None, :]).reshape(-1)
    per_block = dp_count // input_blocks
    place = jnp.stack([half, dp_id, dp_id // per_block, lax.rem(dp_id, per_block)]).astype(jnp.int32)

    swapped = [one, two, three, four]
    in_ring = jnp.stack([p for pair in zip(near_parts, far_parts) for p in pair])
    token_total = jnp.sum(in_ring[:, input_blocks * piece, 0].astype(jnp.float32)).reshape(1)
    in_ring = in_ring[:, : input_blocks * piece].reshape(dp_count, input_blocks, piece, block)
    ordered = (x_order[None, :] * z_count + z_from[:, None]).reshape(-1)
    matches = ordered[None, :] == jnp.arange(dp_count, dtype=jnp.int32)[:, None]
    ring_place = jnp.sum(jnp.where(matches, jnp.arange(dp_count, dtype=jnp.int32)[None, :], 0), axis=1)
    a_inverse = jnp.take(in_ring, ring_place, axis=0).transpose(1, 0, 2, 3).reshape(input_blocks, block, block)

    scale = 1.0 / token_total
    acc, stat1, gram1 = first_part(source, place, in_own, shards, rows, held, slots_here, block)
    preconditioned, output_stats, input_stats = last_part(
        source, place, used_here, scale, in_mir, shards, swapped, acc, stat1, gram1, local_blocks, a_inverse,
        rows, first_late,
    )
    return (preconditioned[None], output_stats[None], input_stats[None])


def solution(mesh):
    in_specs = (
        P("section", "dp", None, None),
        P("section", "dp", None, None),
        P("section", "dp"),
        P("section", "dp", None),
        P("section", None),
        P("section", "dp", None, None),
    )
    out_specs = (
        P("section", "dp", None, None),
        P("section", "dp", None, None),
        P("section", "dp", None),
    )
    return jax.shard_map(local, mesh=mesh, in_specs=in_specs, out_specs=out_specs, check_vma=False)
```

```python
import functools

import jax
import jax.numpy as jnp
from jax import lax
from jax.experimental import pallas as pl
from jax.experimental.pallas import tpu as pltpu
from jax.sharding import PartitionSpec as P

MB = 4
VMEM_BYTES = 56 * 1024 * 1024


def z_step(value, step):
    count = lax.axis_size("dp")
    pairs = [(d, (d + 2 * step) % count) for d in range(count)]
    return lax.ppermute(value, "dp", pairs)


def x_swap(value):
    count = lax.axis_size("dp")
    return lax.ppermute(value, "dp", [(d, d ^ 1) for d in range(count)])


def ring_start(start):
    return z_step(start, 1), z_step(start, -1)


def ring_start_pair(up, down):
    return z_step(up, 1), z_step(down, -1)


def ring_end(up, down):
    cut = up.shape[0] // 2
    return z_step(up[:cut], 1), z_step(down[cut:], -1)


def live_mask(count_live, sizes, rows_total, per_slot):
    index = jnp.arange(rows_total, dtype=jnp.int32)
    group = index // per_slot
    within = index % per_slot
    slot_ids = jnp.arange(sizes.shape[0], dtype=jnp.int32)
    picked = jnp.sum(jnp.where(group[:, None] == slot_ids[None, :], sizes[None, :], 0), axis=1)
    return (group < count_live) & (within < picked)


def contract_rows(first_mat, second_mat):
    return lax.dot_general(
        first_mat, second_mat, (((0,), (0,)), ((), ())), preferred_element_type=jnp.float32
    )


def route_kernel(with_pieces, slots_here, pick, limit, count, g_ref, *rest):
    if with_pieces:
        inv_ref, out_ref = rest
    else:
        (out_ref,) = rest
    rows, width = g_ref.shape
    dests = out_ref.shape[0]
    block = out_ref.shape[2]
    per = rows // MB
    piece = block // dests
    within = lax.broadcasted_iota(jnp.int32, (per, block), 0)
    keep = [within < limit[m] for m in range(MB)]

    @pl.loop(0, dests)
    def _(dest):
        for t in range(slots_here):
            number = pick[dest * slots_here + t]
            start = pl.multiple_of(number * block, block)
            for m in range(MB):
                part = g_ref[pl.ds(m * per, per), pl.ds(start, block)]
                part = jnp.where(keep[m], part, jnp.zeros_like(part))
                out_ref[dest, pl.ds(t * rows + m * per, per), :] = part
            if with_pieces:
                out_ref[dest, pl.ds(slots_here * rows + t * piece, piece), :] = inv_ref[
                    t, pl.ds(pl.multiple_of(dest * piece, piece), piece), :
                ]
        if not with_pieces:
            live = jnp.full((16, block), count[0].astype(jnp.float32))
            out_ref[dest, pl.ds(slots_here * rows, 16), :] = live.astype(out_ref.dtype)


def route(pick, limit, count, g_rows, inverses, dests, slots_here, block):
    rows = slots_here * g_rows.shape[0]
    operands = [g_rows]
    if inverses is not None:
        rows += slots_here * (block // dests)
        operands.append(inverses)
    else:
        rows += 16
    vmem = pl.BlockSpec(memory_space=pltpu.VMEM)
    smem = pl.BlockSpec(memory_space=pltpu.SMEM)
    return pl.pallas_call(
        functools.partial(route_kernel, inverses is not None, slots_here),
        out_shape=jax.ShapeDtypeStruct((dests, rows, block), jnp.bfloat16),
        in_specs=[smem, smem, smem] + [vmem] * len(operands),
        out_specs=vmem,
        compiler_params=pltpu.CompilerParams(vmem_limit_bytes=VMEM_BYTES),
        cost_estimate=pl.CostEstimate(flops=0, bytes_accessed=8 * 2**20, transcendentals=0),
    )(pick, limit, count, *operands)


def pack_routed(rows, source, routed_ref, packed, turned):
    for t in range(turned.shape[0]):
        for n in range(routed_ref.shape[0]):
            packed[t, pl.ds(n * rows, rows), :] = routed_ref[source[n], pl.ds(t * rows, rows), :]
        turned[t] = packed[t].T


def half_columns(packed, t, half, half_block):
    return packed[t, :, pl.ds(pl.multiple_of(half * half_block, half_block), half_block)]


def gram_here(place, xs, width):
    cols = xs[:, pl.ds(pl.multiple_of(place[3] * width, width), width)]
    return jnp.dot(cols.T, xs[...], preferred_element_type=jnp.float32)


def ring_rows(shards, first, count):
    picked = []
    for d in range(4):
        picked.append([(shards[d], first, count)])
    top, bottom = shards[4], shards[5]
    cut = top.shape[0]
    upper = min(max(cut - first, 0), count)
    parts = []
    if upper:
        parts.append((top, first, upper))
    if upper < count:
        parts.append((bottom, first + upper - cut, count - upper))
    picked.append(parts)
    for d in (6, 7, 8):
        picked.append([(shards[d], first, count)])
    return picked


def first_kernel(rows, held, source, place, routed_ref, *refs):
    shards, (acc_ref, stat_ref, gram_ref, packed, turned, xs) = refs[:9], refs[9:]
    k = pl.program_id(0)

    @pl.when(k == 0)
    def _():
        pack_routed(rows, source, routed_ref, packed, turned)
        for t in range(turned.shape[0]):
            cols = half_columns(packed, t, place[0], stat_ref.shape[2])
            stat_ref[t] = jnp.dot(turned[t], cols, preferred_element_type=jnp.float32)

    at = 0
    mine, other = ring_rows(shards, 0, rows), ring_rows(shards, held, rows)
    for d in range(8):
        for ref, start, count in mine[d] + other[d]:
            xs[pl.ds(at, count), :] = ref[pl.ds(start, count), :]
            at += count
    both = turned[...].reshape(-1, turned.shape[2])
    grad = jnp.dot(both, xs[...], preferred_element_type=jnp.float32)
    acc_ref[...] = grad.reshape(acc_ref.shape)

    @pl.when(k == place[2])
    def _():
        gram_ref[...] = gram_here(place, xs, gram_ref.shape[0])


def column_spec(array, block):
    return pl.BlockSpec((array.shape[0], block), lambda k: (0, k))


def first_part(source, place, routed, shards, rows, held, slots_here, block):
    width = shards[0].shape[1]
    tokens = routed.shape[0] * rows
    gram_rows = width // routed.shape[0]
    vmem = pl.BlockSpec(memory_space=pltpu.VMEM)
    smem = pl.BlockSpec(memory_space=pltpu.SMEM)
    flops = 2 * slots_here * block * tokens * (width + block // 2)
    return pl.pallas_call(
        functools.partial(first_kernel, rows, held),
        grid=(width // block,),
        out_shape=(
            jax.ShapeDtypeStruct((slots_here, block, width), jnp.float32),
            jax.ShapeDtypeStruct((slots_here, block, block // 2), jnp.float32),
            jax.ShapeDtypeStruct((gram_rows, block), jnp.float32),
        ),
        in_specs=[smem, smem, vmem] + [column_spec(s, block) for s in shards],
        out_specs=(
            pl.BlockSpec((slots_here, block, block), lambda k: (0, 0, k)),
            pl.BlockSpec((slots_here, block, block // 2), lambda k: (0, 0, 0)),
            pl.BlockSpec((gram_rows, block), lambda k: (0, 0)),
        ),
        scratch_shapes=[
            pltpu.VMEM((slots_here, tokens, block), jnp.bfloat16),
            pltpu.VMEM((slots_here, block, tokens), jnp.bfloat16),
            pltpu.VMEM((tokens, block), jnp.bfloat16),
        ],
        compiler_params=pltpu.CompilerParams(vmem_limit_bytes=VMEM_BYTES),
        cost_estimate=pl.CostEstimate(flops=flops, bytes_accessed=16 * 2**20, transcendentals=0),
    )(source, place, routed, *shards)


def last_kernel(rows, first_late, source, place, used, routed_ref, *refs):
    shards, swapped = refs[:9], refs[9:14]
    acc_ref, stat1_ref, gram1_ref, inv_ref, out_ref, stat_ref, gram_ref, packed, turned, xs, a_mat, scale, left_both = refs[14:]
    k = pl.program_id(0)

    @pl.when(k == 0)
    def _():
        total = jnp.zeros(scale.shape, jnp.float32)
        for n in range(routed_ref.shape[0]):
            total += routed_ref[n, pl.ds(turned.shape[0] * rows, scale.shape[0]), :].astype(jnp.float32)
        scale[...] = 1.0 / total
        pack_routed(rows, source, routed_ref, packed, turned)
        for t in range(turned.shape[0]):
            cols = half_columns(packed, t, place[0], stat_ref.shape[2])
            stat = stat1_ref[t] + jnp.dot(turned[t], cols, preferred_element_type=jnp.float32)
            stat = stat * scale[:1, : stat.shape[1]]
            stat_ref[t] = jnp.where(used[t] > 0, stat, 0.0).astype(stat_ref.dtype)

    zero, one, two, three, four = swapped
    late = four.shape[0]
    partner = [(zero, 0), (one, 0), (two, 0), (three, 0), (four, 0), (three, 1), (two, 1), (one, 1)]
    mine = ring_rows(shards, first_late, rows)
    pieces = ring_rows(shards, first_late + rows, late - rows)
    piece = a_mat.shape[0] // 16
    at = 0
    for d in range(8):
        ref, number = partner[d]
        for part, start, count in mine[d] + [(ref, number * late, rows)]:
            xs[pl.ds(at, count), :] = part[pl.ds(start, count), :]
            at += count
        for n, found in enumerate([pieces[d], [(ref, number * late + rows, piece)]]):
            to = pl.multiple_of(source[2 * d + n] * piece, piece)
            for part, start, count in found:
                a_mat[pl.ds(to, count), :] = part[pl.ds(start, count), :]
                to += count

    slots_here, block, tokens = turned.shape
    both = turned[...].reshape(slots_here * block, tokens)
    grads = jnp.dot(both, xs[...], preferred_element_type=jnp.float32)
    for t in range(slots_here):
        grad = acc_ref[t] + grads[t * block : (t + 1) * block]
        grad = (grad * scale[:1]).astype(jnp.bfloat16)
        left = jnp.dot(inv_ref[t], grad, preferred_element_type=jnp.float32)
        left_both[pl.ds(t * block, block), :] = left.astype(jnp.bfloat16)
    scaled = jnp.dot(left_both[...], a_mat[...], preferred_element_type=jnp.float32)
    for t in range(slots_here):
        part = scaled[t * block : (t + 1) * block]
        out_ref[t] = jnp.where(used[t] > 0, part, 0.0).astype(out_ref.dtype)

    @pl.when(k == place[2])
    def _():
        gram_ref[...] = (gram1_ref[...] + gram_here(place, xs, gram_ref.shape[0])) * scale[:1]


def last_part(source, place, used, routed, shards, swapped, acc, stat1, gram1, inverses, rows, first_late):
    width = acc.shape[2]
    slots_here, block = inverses.shape[:2]
    tokens = routed.shape[0] * rows
    vmem = pl.BlockSpec(memory_space=pltpu.VMEM)
    smem = pl.BlockSpec(memory_space=pltpu.SMEM)
    flops = 2 * slots_here * block * width * (tokens + 2 * block)
    return pl.pallas_call(
        functools.partial(last_kernel, rows, first_late),
        grid=(width // block,),
        out_shape=(
            jax.ShapeDtypeStruct((slots_here, block, width), jnp.bfloat16),
            jax.ShapeDtypeStruct((slots_here, block, block // 2), jnp.bfloat16),
            jax.ShapeDtypeStruct(gram1.shape, jnp.float32),
        ),
        in_specs=[smem, smem, smem, vmem]
        + [column_spec(s, block) for s in list(shards) + list(swapped)]
        + [
            pl.BlockSpec((slots_here, block, block), lambda k: (0, 0, k)), vmem, vmem, vmem,
        ],
        out_specs=(
            pl.BlockSpec((slots_here, block, block), lambda k: (0, 0, k)),
            pl.BlockSpec((slots_here, block, block // 2), lambda k: (0, 0, 0)),
            pl.BlockSpec(gram1.shape, lambda k: (0, 0)),
        ),
        scratch_shapes=[
            pltpu.VMEM((slots_here, tokens, block), jnp.bfloat16),
            pltpu.VMEM((slots_here, block, tokens), jnp.bfloat16),
            pltpu.VMEM((tokens, block), jnp.bfloat16),
            pltpu.VMEM((block, block), jnp.bfloat16),
            pltpu.VMEM((16, block), jnp.float32),
            pltpu.VMEM((slots_here * block, block), jnp.bfloat16),
        ],
        compiler_params=pltpu.CompilerParams(vmem_limit_bytes=VMEM_BYTES),
        cost_estimate=pl.CostEstimate(flops=flops, bytes_accessed=24 * 2**20, transcendentals=0),
    )(source, place, used, routed, *shards, *swapped, acc, stat1, gram1, inverses)


def local(activations, cotangents, mb_count, mb_size, block_slot, inv_blocks):
    rows = activations.shape[2]
    width = activations.shape[3]
    hidden_width = cotangents.shape[3]
    block = inv_blocks.shape[2]
    slots_here = inv_blocks.shape[1]
    half_width = width // 2
    hidden_blocks = hidden_width // block
    input_blocks = half_width // block
    section_count = lax.axis_size("section")
    dp_count = lax.axis_size("dp")
    section_id = lax.axis_index("section")
    dp_id = lax.axis_index("dp")
    half = (section_id >= section_count // 2).astype(jnp.int32)
    zero_bf = jnp.zeros((), jnp.bfloat16)
    mirror = [(s, section_count - 1 - s) for s in range(section_count)]

    x_all = activations[0, 0]
    g_raw = cotangents[0, 0]
    local_blocks = inv_blocks[0]
    meta = jnp.concatenate([mb_count[0], mb_size[0, 0]])
    x_sent = lax.dynamic_slice_in_dim(x_all, (1 - half) * half_width, half_width, 1)
    g_m = lax.ppermute(g_raw, "section", mirror)

    def limits(numbers):
        return jnp.where(jnp.arange(MB, dtype=jnp.int32) < numbers[0], numbers[1:], 0)

    slot_table = block_slot[0]
    hidden_table = slot_table[:hidden_blocks]
    input_table = slot_table[hidden_blocks:]
    hidden_ids = jnp.arange(hidden_blocks, dtype=jnp.int32)
    every_slot = jnp.arange(dp_count * slots_here, dtype=jnp.int32)
    slot_matches = hidden_table[None, :] == every_slot[:, None]
    block_pick = jnp.sum(jnp.where(slot_matches, hidden_ids[None, :], 0), axis=1)
    my_slots = dp_id * slots_here + jnp.arange(slots_here, dtype=jnp.int32)
    used_here = jnp.any(hidden_table[None, :] == my_slots[:, None], axis=1).astype(jnp.int32)

    live_own = live_mask(meta[0], meta[1:], rows, rows // MB)
    x_own = lax.dynamic_slice_in_dim(x_all, half * half_width, half_width, 1)
    x_own = jnp.where(live_own[:, None], x_own, zero_bf)
    out_own = route(block_pick, limits(meta), jnp.zeros((1,), jnp.int32), g_raw, local_blocks, dp_count, slots_here, block)
    x_far, out_own, meta_sent, x_sent, g_sent = lax.optimization_barrier((x_swap(x_own), out_own, meta, x_sent, g_raw))
    meta_m = lax.ppermute(meta_sent, "section", mirror)
    x_m = lax.ppermute(x_sent, "section", mirror)
    g_m = lax.ppermute(g_sent, "section", mirror)
    live_mir = live_mask(meta_m[0], meta_m[1:], rows, rows // MB)
    count = jnp.sum(live_own.astype(jnp.int32)) + jnp.sum(live_mir.astype(jnp.int32))
    x_mir = jnp.where(live_mir[:, None], x_m, zero_bf)
    own0 = jnp.concatenate([x_own, x_far], axis=0)

    in_own = lax.all_to_all(out_own, "dp", split_axis=0, concat_axis=0, tiled=True)
    own_up1, own_down1 = ring_start(own0)
    own_up1, own_down1, in_own, g_m = lax.optimization_barrier((own_up1, own_down1, in_own, g_m))

    piece = block // dp_count
    pieces = in_own[:, slots_here * rows :].reshape(dp_count * slots_here, piece, block)
    mine = jnp.take(pieces, input_table, axis=0).transpose(1, 0, 2).reshape(piece, half_width)
    mir0 = jnp.concatenate([x_mir, mine], axis=0)
    up1, down1 = ring_start(mir0)
    zero = x_swap(mir0)
    own_up2, own_down2 = ring_start_pair(own_up1, own_down1)
    up1, down1, own_up2, own_down2, zero = lax.optimization_barrier((up1, down1, own_up2, own_down2, zero))
    one = x_swap(jnp.concatenate([up1, down1], axis=0))
    up2, down2 = ring_start_pair(up1, down1)
    own_up3, own_down3 = ring_start_pair(own_up2, own_down2)
    out_mir = route(block_pick, limits(meta_m), count.reshape(1), g_m, None, dp_count, slots_here, block)
    up2, down2, own_up3, own_down3, out_mir = lax.optimization_barrier((up2, down2, own_up3, own_down3, out_mir))
    two = x_swap(jnp.concatenate([up2, down2], axis=0))
    up3, down3 = ring_start_pair(up2, down2)
    own_top4, own_bottom4 = ring_end(own_up3, own_down3)
    up3, down3, own_top4, own_bottom4, one = lax.optimization_barrier((up3, down3, own_top4, own_bottom4, one))
    three = x_swap(jnp.concatenate([up3, down3], axis=0))
    top4, bottom4 = ring_end(up3, down3)
    top4, bottom4, out_mir, two = lax.optimization_barrier((top4, bottom4, out_mir, two))
    four = x_swap(jnp.concatenate([top4, bottom4], axis=0))
    own_shards = [own0, own_up1, own_up2, own_up3, own_top4, own_bottom4, own_down3, own_down2, own_down1]
    shards = [mir0, up1, up2, up3, top4, bottom4, down3, down2, down1]

    in_mir = lax.all_to_all(out_mir, "dp", split_axis=0, concat_axis=0, tiled=True)

    z_count = dp_count // 2
    z_from = lax.rem(dp_id // 2 - jnp.arange(z_count, dtype=jnp.int32) + z_count, z_count)
    x_here = lax.rem(dp_id, 2)
    x_order = jnp.stack([x_here, 1 - x_here])
    source = (z_from[:, None] * 2 + x_order[None, :]).reshape(-1)
    per_block = dp_count // input_blocks
    place = jnp.stack([half, dp_id, dp_id // per_block, lax.rem(dp_id, per_block)]).astype(jnp.int32)

    swapped = [zero, one, two, three, four]
    acc, stat1, gram1 = first_part(source, place, in_own, own_shards, rows, rows, slots_here, block)
    preconditioned, output_stats, input_stats = last_part(
        source, place, used_here, in_mir, shards, swapped, acc, stat1, gram1, local_blocks,
        rows, 0,
    )
    return (preconditioned[None], output_stats[None], input_stats[None])


def solution(mesh):
    in_specs = (
        P("section", "dp", None, None),
        P("section", "dp", None, None),
        P("section", "dp"),
        P("section", "dp", None),
        P("section", None),
        P("section", "dp", None, None),
    )
    out_specs = (
        P("section", "dp", None, None),
        P("section", "dp", None, None),
        P("section", "dp", None),
    )
    return jax.shard_map(local, mesh=mesh, in_specs=in_specs, out_specs=out_specs, check_vma=False)
```

```python
import functools

import jax
import jax.numpy as jnp
from jax import lax
from jax.experimental import pallas as pl
from jax.experimental.pallas import tpu as pltpu
from jax.sharding import PartitionSpec as P

MB = 4
VMEM_BYTES = 56 * 1024 * 1024


def z_step(value, step):
    count = lax.axis_size("dp")
    pairs = [(d, (d + 2 * step) % count) for d in range(count)]
    return lax.ppermute(value, "dp", pairs)


def x_swap(value):
    count = lax.axis_size("dp")
    return lax.ppermute(value, "dp", [(d, d ^ 1) for d in range(count)])


def ring_start(start):
    return z_step(start, 1), z_step(start, -1)


def ring_start_pair(up, down):
    return z_step(up, 1), z_step(down, -1)


def ring_end(up, down):
    cut = up.shape[0] // 2
    return z_step(up[:cut], 1), z_step(down[cut:], -1)


def live_mask(count_live, sizes, rows_total, per_slot):
    index = jnp.arange(rows_total, dtype=jnp.int32)
    group = index // per_slot
    within = index % per_slot
    slot_ids = jnp.arange(sizes.shape[0], dtype=jnp.int32)
    picked = jnp.sum(jnp.where(group[:, None] == slot_ids[None, :], sizes[None, :], 0), axis=1)
    return (group < count_live) & (within < picked)


def contract_rows(first_mat, second_mat):
    return lax.dot_general(
        first_mat, second_mat, (((0,), (0,)), ((), ())), preferred_element_type=jnp.float32
    )


def route_kernel(with_pieces, slots_here, pick, limit, count, g_ref, *rest):
    if with_pieces:
        inv_ref, out_ref = rest
    else:
        (out_ref,) = rest
    rows, width = g_ref.shape
    dests = out_ref.shape[0]
    block = out_ref.shape[2]
    per = rows // MB
    piece = block // dests
    within = lax.broadcasted_iota(jnp.int32, (per, block), 0)
    keep = [within < limit[m] for m in range(MB)]

    @pl.loop(0, dests)
    def _(dest):
        for t in range(slots_here):
            number = pick[dest * slots_here + t]
            start = pl.multiple_of(number * block, block)
            for m in range(MB):
                part = g_ref[pl.ds(m * per, per), pl.ds(start, block)]
                part = jnp.where(keep[m], part, jnp.zeros_like(part))
                out_ref[dest, pl.ds(t * rows + m * per, per), :] = part
            if with_pieces:
                out_ref[dest, pl.ds(slots_here * rows + t * piece, piece), :] = inv_ref[
                    t, pl.ds(pl.multiple_of(dest * piece, piece), piece), :
                ]
        if not with_pieces:
            live = jnp.full((16, block), count[0].astype(jnp.float32))
            out_ref[dest, pl.ds(slots_here * rows, 16), :] = live.astype(out_ref.dtype)


def route(pick, limit, count, g_rows, inverses, dests, slots_here, block):
    rows = slots_here * g_rows.shape[0]
    operands = [g_rows]
    if inverses is not None:
        rows += slots_here * (block // dests)
        operands.append(inverses)
    else:
        rows += 16
    vmem = pl.BlockSpec(memory_space=pltpu.VMEM)
    smem = pl.BlockSpec(memory_space=pltpu.SMEM)
    return pl.pallas_call(
        functools.partial(route_kernel, inverses is not None, slots_here),
        out_shape=jax.ShapeDtypeStruct((dests, rows, block), jnp.bfloat16),
        in_specs=[smem, smem, smem] + [vmem] * len(operands),
        out_specs=vmem,
        compiler_params=pltpu.CompilerParams(vmem_limit_bytes=VMEM_BYTES),
        cost_estimate=pl.CostEstimate(flops=0, bytes_accessed=8 * 2**20, transcendentals=0),
    )(pick, limit, count, *operands)


def pack_routed(rows, source, routed_ref, packed, turned):
    for t in range(turned.shape[0]):
        for n in range(routed_ref.shape[0]):
            packed[t, pl.ds(n * rows, rows), :] = routed_ref[source[n], pl.ds(t * rows, rows), :]
        turned[t] = packed[t].T


def half_columns(packed, t, half, half_block):
    return packed[t, :, pl.ds(pl.multiple_of(half * half_block, half_block), half_block)]


def gram_here(place, xs, width):
    cols = xs[:, pl.ds(pl.multiple_of(place[3] * width, width), width)]
    return jnp.dot(cols.T, xs[...], preferred_element_type=jnp.float32)


def ring_rows(shards, first, count):
    picked = []
    for d in range(4):
        picked.append([(shards[d], first, count)])
    top, bottom = shards[4], shards[5]
    cut = top.shape[0]
    upper = min(max(cut - first, 0), count)
    parts = []
    if upper:
        parts.append((top, first, upper))
    if upper < count:
        parts.append((bottom, first + upper - cut, count - upper))
    picked.append(parts)
    for d in (6, 7, 8):
        picked.append([(shards[d], first, count)])
    return picked


def first_kernel(rows, held, source, place, routed_ref, *refs):
    shards, (acc_ref, stat_ref, gram_ref, packed, turned, xs) = refs[:9], refs[9:]
    k = pl.program_id(0)

    @pl.when(k == 0)
    def _():
        pack_routed(rows, source, routed_ref, packed, turned)
        for t in range(turned.shape[0]):
            cols = half_columns(packed, t, place[0], stat_ref.shape[2])
            stat_ref[t] = jnp.dot(turned[t], cols, preferred_element_type=jnp.float32)

    at = 0
    mine, other = ring_rows(shards, 0, rows), ring_rows(shards, held, rows)
    for d in range(8):
        for ref, start, count in mine[d] + other[d]:
            xs[pl.ds(at, count), :] = ref[pl.ds(start, count), :]
            at += count
    both = turned[...].reshape(-1, turned.shape[2])
    grad = jnp.dot(both, xs[...], preferred_element_type=jnp.float32)
    acc_ref[...] = grad.reshape(acc_ref.shape)

    @pl.when(k == place[2])
    def _():
        gram_ref[...] = gram_here(place, xs, gram_ref.shape[0])


def column_spec(array, block):
    return pl.BlockSpec((array.shape[0], block), lambda k: (0, k))


def first_part(source, place, routed, shards, rows, held, slots_here, block):
    width = shards[0].shape[1]
    tokens = routed.shape[0] * rows
    gram_rows = width // routed.shape[0]
    vmem = pl.BlockSpec(memory_space=pltpu.VMEM)
    smem = pl.BlockSpec(memory_space=pltpu.SMEM)
    flops = 2 * slots_here * block * tokens * (width + block // 2)
    return pl.pallas_call(
        functools.partial(first_kernel, rows, held),
        grid=(width // block,),
        out_shape=(
            jax.ShapeDtypeStruct((slots_here, block, width), jnp.float32),
            jax.ShapeDtypeStruct((slots_here, block, block // 2), jnp.float32),
            jax.ShapeDtypeStruct((gram_rows, block), jnp.float32),
        ),
        in_specs=[smem, smem, vmem] + [column_spec(s, block) for s in shards],
        out_specs=(
            pl.BlockSpec((slots_here, block, block), lambda k: (0, 0, k)),
            pl.BlockSpec((slots_here, block, block // 2), lambda k: (0, 0, 0)),
            pl.BlockSpec((gram_rows, block), lambda k: (0, 0)),
        ),
        scratch_shapes=[
            pltpu.VMEM((slots_here, tokens, block), jnp.bfloat16),
            pltpu.VMEM((slots_here, block, tokens), jnp.bfloat16),
            pltpu.VMEM((tokens, block), jnp.bfloat16),
        ],
        compiler_params=pltpu.CompilerParams(vmem_limit_bytes=VMEM_BYTES),
        cost_estimate=pl.CostEstimate(flops=flops, bytes_accessed=16 * 2**20, transcendentals=0),
    )(source, place, routed, *shards)


def last_kernel(rows, first_late, source, place, used, routed_ref, *refs):
    shards, swapped = refs[:9], refs[9:14]
    acc_ref, stat1_ref, gram1_ref, inv_ref, out_ref, stat_ref, gram_ref, packed, turned, xs, a_mat, scale, left_both = refs[14:]
    k = pl.program_id(0)

    @pl.when(k == 0)
    def _():
        total = jnp.zeros(scale.shape, jnp.float32)
        for n in range(routed_ref.shape[0]):
            total += routed_ref[n, pl.ds(turned.shape[0] * rows, scale.shape[0]), :].astype(jnp.float32)
        scale[...] = 1.0 / total
        pack_routed(rows, source, routed_ref, packed, turned)
        for t in range(turned.shape[0]):
            cols = half_columns(packed, t, place[0], stat_ref.shape[2])
            stat = stat1_ref[t] + jnp.dot(turned[t], cols, preferred_element_type=jnp.float32)
            stat = stat * scale[:1, : stat.shape[1]]
            stat_ref[t] = jnp.where(used[t] > 0, stat, 0.0).astype(stat_ref.dtype)

    zero, one, two, three, four = swapped
    late = four.shape[0]
    partner = [(zero, 0), (one, 0), (two, 0), (three, 0), (four, 0), (three, 1), (two, 1), (one, 1)]
    mine = ring_rows(shards, first_late, rows)
    pieces = ring_rows(shards, first_late + rows, late - rows)
    piece = a_mat.shape[0] // 16
    at = 0
    for d in range(8):
        ref, number = partner[d]
        for part, start, count in mine[d] + [(ref, number * late, rows)]:
            xs[pl.ds(at, count), :] = part[pl.ds(start, count), :]
            at += count
        for n, found in enumerate([pieces[d], [(ref, number * late + rows, piece)]]):
            to = pl.multiple_of(source[2 * d + n] * piece, piece)
            for part, start, count in found:
                a_mat[pl.ds(to, count), :] = part[pl.ds(start, count), :]
                to += count

    slots_here, block, tokens = turned.shape
    both = turned[...].reshape(slots_here * block, tokens)
    grads = jnp.dot(both, xs[...], preferred_element_type=jnp.float32)
    for t in range(slots_here):
        grad = acc_ref[t] + grads[t * block : (t + 1) * block]
        grad = (grad * scale[:1]).astype(jnp.bfloat16)
        left = jnp.dot(inv_ref[t], grad, preferred_element_type=jnp.float32)
        left_both[pl.ds(t * block, block), :] = left.astype(jnp.bfloat16)
    scaled = jnp.dot(left_both[...], a_mat[...], preferred_element_type=jnp.float32)
    for t in range(slots_here):
        part = scaled[t * block : (t + 1) * block]
        out_ref[t] = jnp.where(used[t] > 0, part, 0.0).astype(out_ref.dtype)

    @pl.when(k == place[2])
    def _():
        gram_ref[...] = (gram1_ref[...] + gram_here(place, xs, gram_ref.shape[0])) * scale[:1]


def last_part(source, place, used, routed, shards, swapped, acc, stat1, gram1, inverses, rows, first_late):
    width = acc.shape[2]
    slots_here, block = inverses.shape[:2]
    tokens = routed.shape[0] * rows
    vmem = pl.BlockSpec(memory_space=pltpu.VMEM)
    smem = pl.BlockSpec(memory_space=pltpu.SMEM)
    flops = 2 * slots_here * block * width * (tokens + 2 * block)
    return pl.pallas_call(
        functools.partial(last_kernel, rows, first_late),
        grid=(width // block,),
        out_shape=(
            jax.ShapeDtypeStruct((slots_here, block, width), jnp.bfloat16),
            jax.ShapeDtypeStruct((slots_here, block, block // 2), jnp.bfloat16),
            jax.ShapeDtypeStruct(gram1.shape, jnp.float32),
        ),
        in_specs=[smem, smem, smem, vmem]
        + [column_spec(s, block) for s in list(shards) + list(swapped)]
        + [
            pl.BlockSpec((slots_here, block, block), lambda k: (0, 0, k)), vmem, vmem, vmem,
        ],
        out_specs=(
            pl.BlockSpec((slots_here, block, block), lambda k: (0, 0, k)),
            pl.BlockSpec((slots_here, block, block // 2), lambda k: (0, 0, 0)),
            pl.BlockSpec(gram1.shape, lambda k: (0, 0)),
        ),
        scratch_shapes=[
            pltpu.VMEM((slots_here, tokens, block), jnp.bfloat16),
            pltpu.VMEM((slots_here, block, tokens), jnp.bfloat16),
            pltpu.VMEM((tokens, block), jnp.bfloat16),
            pltpu.VMEM((block, block), jnp.bfloat16),
            pltpu.VMEM((16, block), jnp.float32),
            pltpu.VMEM((slots_here * block, block), jnp.bfloat16),
        ],
        compiler_params=pltpu.CompilerParams(vmem_limit_bytes=VMEM_BYTES),
        cost_estimate=pl.CostEstimate(flops=flops, bytes_accessed=24 * 2**20, transcendentals=0),
    )(source, place, used, routed, *shards, *swapped, acc, stat1, gram1, inverses)


def local(activations, cotangents, mb_count, mb_size, block_slot, inv_blocks):
    rows = activations.shape[2]
    width = activations.shape[3]
    hidden_width = cotangents.shape[3]
    block = inv_blocks.shape[2]
    slots_here = inv_blocks.shape[1]
    half_width = width // 2
    hidden_blocks = hidden_width // block
    input_blocks = half_width // block
    section_count = lax.axis_size("section")
    dp_count = lax.axis_size("dp")
    section_id = lax.axis_index("section")
    dp_id = lax.axis_index("dp")
    half = (section_id >= section_count // 2).astype(jnp.int32)
    zero_bf = jnp.zeros((), jnp.bfloat16)
    mirror = [(s, section_count - 1 - s) for s in range(section_count)]

    x_all = activations[0, 0]
    g_raw = cotangents[0, 0]
    local_blocks = inv_blocks[0]
    meta = jnp.concatenate([mb_count[0], mb_size[0, 0]])
    x_sent = lax.dynamic_slice_in_dim(x_all, (1 - half) * half_width, half_width, 1)

    def limits(numbers):
        return jnp.where(jnp.arange(MB, dtype=jnp.int32) < numbers[0], numbers[1:], 0)

    slot_table = block_slot[0]
    hidden_table = slot_table[:hidden_blocks]
    input_table = slot_table[hidden_blocks:]
    hidden_ids = jnp.arange(hidden_blocks, dtype=jnp.int32)
    every_slot = jnp.arange(dp_count * slots_here, dtype=jnp.int32)
    slot_matches = hidden_table[None, :] == every_slot[:, None]
    block_pick = jnp.sum(jnp.where(slot_matches, hidden_ids[None, :], 0), axis=1)
    my_slots = dp_id * slots_here + jnp.arange(slots_here, dtype=jnp.int32)
    used_here = jnp.any(hidden_table[None, :] == my_slots[:, None], axis=1).astype(jnp.int32)

    live_own = live_mask(meta[0], meta[1:], rows, rows // MB)
    x_own = lax.dynamic_slice_in_dim(x_all, half * half_width, half_width, 1)
    x_own = jnp.where(live_own[:, None], x_own, zero_bf)
    out_own = route(block_pick, limits(meta), jnp.zeros((1,), jnp.int32), g_raw, local_blocks, dp_count, slots_here, block)
    x_far, out_own, meta_sent, x_sent, g_sent = lax.optimization_barrier((x_swap(x_own), out_own, meta, x_sent, g_raw))
    meta_m = lax.ppermute(meta_sent, "section", mirror)
    x_m = lax.ppermute(x_sent, "section", mirror)
    g_m = lax.ppermute(g_sent, "section", mirror)
    live_mir = live_mask(meta_m[0], meta_m[1:], rows, rows // MB)
    count = jnp.sum(live_own.astype(jnp.int32)) + jnp.sum(live_mir.astype(jnp.int32))
    x_mir = jnp.where(live_mir[:, None], x_m, zero_bf)
    own0 = jnp.concatenate([x_own, x_far], axis=0)

    in_own = lax.all_to_all(out_own, "dp", split_axis=0, concat_axis=0, tiled=True)
    own_up1, own_down1 = ring_start(own0)

    piece = block // dp_count
    pieces = in_own[:, slots_here * rows :].reshape(dp_count * slots_here, piece, block)
    mine = jnp.take(pieces, input_table, axis=0).transpose(1, 0, 2).reshape(piece, half_width)
    mir0 = jnp.concatenate([x_mir, mine], axis=0)
    up1, down1 = ring_start(mir0)
    zero = x_swap(mir0)
    own_up2, own_down2 = ring_start_pair(own_up1, own_down1)
    up1, down1, own_up2, own_down2, zero, g_m = lax.optimization_barrier((up1, down1, own_up2, own_down2, zero, g_m))
    one = x_swap(jnp.concatenate([up1, down1], axis=0))
    up2, down2 = ring_start_pair(up1, down1)
    own_up3, own_down3 = ring_start_pair(own_up2, own_down2)
    out_mir = route(block_pick, limits(meta_m), count.reshape(1), g_m, None, dp_count, slots_here, block)
    up2, down2, own_up3, own_down3, out_mir = lax.optimization_barrier((up2, down2, own_up3, own_down3, out_mir))
    two = x_swap(jnp.concatenate([up2, down2], axis=0))
    up3, down3 = ring_start_pair(up2, down2)
    own_top4, own_bottom4 = ring_end(own_up3, own_down3)
    up3, down3, own_top4, own_bottom4, one = lax.optimization_barrier((up3, down3, own_top4, own_bottom4, one))
    three = x_swap(jnp.concatenate([up3, down3], axis=0))
    top4, bottom4 = ring_end(up3, down3)
    top4, bottom4, out_mir, two = lax.optimization_barrier((top4, bottom4, out_mir, two))
    four = x_swap(jnp.concatenate([top4, bottom4], axis=0))
    own_shards = [own0, own_up1, own_up2, own_up3, own_top4, own_bottom4, own_down3, own_down2, own_down1]
    shards = [mir0, up1, up2, up3, top4, bottom4, down3, down2, down1]

    in_mir = lax.all_to_all(out_mir, "dp", split_axis=0, concat_axis=0, tiled=True)

    z_count = dp_count // 2
    z_from = lax.rem(dp_id // 2 - jnp.arange(z_count, dtype=jnp.int32) + z_count, z_count)
    x_here = lax.rem(dp_id, 2)
    x_order = jnp.stack([x_here, 1 - x_here])
    source = (z_from[:, None] * 2 + x_order[None, :]).reshape(-1)
    per_block = dp_count // input_blocks
    place = jnp.stack([half, dp_id, dp_id // per_block, lax.rem(dp_id, per_block)]).astype(jnp.int32)

    swapped = [zero, one, two, three, four]
    acc, stat1, gram1 = first_part(source, place, in_own, own_shards, rows, rows, slots_here, block)
    preconditioned, output_stats, input_stats = last_part(
        source, place, used_here, in_mir, shards, swapped, acc, stat1, gram1, local_blocks,
        rows, 0,
    )
    return (preconditioned[None], output_stats[None], input_stats[None])


def solution(mesh):
    in_specs = (
        P("section", "dp", None, None),
        P("section", "dp", None, None),
        P("section", "dp"),
        P("section", "dp", None),
        P("section", None),
        P("section", "dp", None, None),
    )
    out_specs = (
        P("section", "dp", None, None),
        P("section", "dp", None, None),
        P("section", "dp", None),
    )
    return jax.shard_map(local, mesh=mesh, in_specs=in_specs, out_specs=out_specs, check_vma=False)
```

```python
import functools

import jax
import jax.numpy as jnp
from jax import lax
from jax.experimental import pallas as pl
from jax.experimental.pallas import tpu as pltpu
from jax.sharding import PartitionSpec as P

MB = 4
VMEM_BYTES = 56 * 1024 * 1024


def z_step(value, step):
    count = lax.axis_size("dp")
    pairs = [(d, (d + 2 * step) % count) for d in range(count)]
    return lax.ppermute(value, "dp", pairs)


def x_swap(value):
    count = lax.axis_size("dp")
    return lax.ppermute(value, "dp", [(d, d ^ 1) for d in range(count)])


def ring_start(start):
    return z_step(start, 1), z_step(start, -1)


def ring_start_pair(up, down):
    return z_step(up, 1), z_step(down, -1)


def ring_end(up, down):
    cut = up.shape[0] // 2
    return z_step(up[:cut], 1), z_step(down[cut:], -1)


def live_mask(count_live, sizes, rows_total, per_slot):
    index = jnp.arange(rows_total, dtype=jnp.int32)
    group = index // per_slot
    within = index % per_slot
    slot_ids = jnp.arange(sizes.shape[0], dtype=jnp.int32)
    picked = jnp.sum(jnp.where(group[:, None] == slot_ids[None, :], sizes[None, :], 0), axis=1)
    return (group < count_live) & (within < picked)


def contract_rows(first_mat, second_mat):
    return lax.dot_general(
        first_mat, second_mat, (((0,), (0,)), ((), ())), preferred_element_type=jnp.float32
    )


def route_kernel(with_pieces, slots_here, pick, limit, count, g_ref, *rest):
    if with_pieces:
        inv_ref, out_ref = rest
    else:
        (out_ref,) = rest
    rows, width = g_ref.shape
    dests = out_ref.shape[0]
    block = out_ref.shape[2]
    per = rows // MB
    piece = block // dests
    within = lax.broadcasted_iota(jnp.int32, (per, block), 0)
    keep = [within < limit[m] for m in range(MB)]

    @pl.loop(0, dests)
    def _(dest):
        for t in range(slots_here):
            number = pick[dest * slots_here + t]
            start = pl.multiple_of(number * block, block)
            for m in range(MB):
                part = g_ref[pl.ds(m * per, per), pl.ds(start, block)]
                part = jnp.where(keep[m], part, jnp.zeros_like(part))
                out_ref[dest, pl.ds(t * rows + m * per, per), :] = part
            if with_pieces:
                out_ref[dest, pl.ds(slots_here * rows + t * piece, piece), :] = inv_ref[
                    t, pl.ds(pl.multiple_of(dest * piece, piece), piece), :
                ]
        if not with_pieces:
            live = jnp.full((16, block), count[0].astype(jnp.float32))
            out_ref[dest, pl.ds(slots_here * rows, 16), :] = live.astype(out_ref.dtype)


def route(pick, limit, count, g_rows, inverses, dests, slots_here, block):
    rows = slots_here * g_rows.shape[0]
    operands = [g_rows]
    if inverses is not None:
        rows += slots_here * (block // dests)
        operands.append(inverses)
    else:
        rows += 16
    vmem = pl.BlockSpec(memory_space=pltpu.VMEM)
    smem = pl.BlockSpec(memory_space=pltpu.SMEM)
    return pl.pallas_call(
        functools.partial(route_kernel, inverses is not None, slots_here),
        out_shape=jax.ShapeDtypeStruct((dests, rows, block), jnp.bfloat16),
        in_specs=[smem, smem, smem] + [vmem] * len(operands),
        out_specs=vmem,
        compiler_params=pltpu.CompilerParams(vmem_limit_bytes=VMEM_BYTES),
        cost_estimate=pl.CostEstimate(flops=0, bytes_accessed=8 * 2**20, transcendentals=0),
    )(pick, limit, count, *operands)


def pack_routed(rows, source, routed_ref, packed, turned):
    for t in range(turned.shape[0]):
        for n in range(routed_ref.shape[0]):
            packed[t, pl.ds(n * rows, rows), :] = routed_ref[source[n], pl.ds(t * rows, rows), :]
        turned[t] = packed[t].T


def half_columns(packed, t, half, half_block):
    return packed[t, :, pl.ds(pl.multiple_of(half * half_block, half_block), half_block)]


def gram_here(place, xs, width):
    cols = xs[:, pl.ds(pl.multiple_of(place[3] * width, width), width)]
    return jnp.dot(cols.T, xs[...], preferred_element_type=jnp.float32)


def ring_rows(shards, first, count):
    picked = []
    for d in range(4):
        picked.append([(shards[d], first, count)])
    top, bottom = shards[4], shards[5]
    cut = top.shape[0]
    upper = min(max(cut - first, 0), count)
    parts = []
    if upper:
        parts.append((top, first, upper))
    if upper < count:
        parts.append((bottom, first + upper - cut, count - upper))
    picked.append(parts)
    for d in (6, 7, 8):
        picked.append([(shards[d], first, count)])
    return picked


def first_kernel(rows, held, source, place, routed_ref, *refs):
    shards, (acc_ref, stat_ref, gram_ref, packed, turned, xs) = refs[:9], refs[9:]
    k = pl.program_id(0)

    @pl.when(k == 0)
    def _():
        pack_routed(rows, source, routed_ref, packed, turned)
        for t in range(turned.shape[0]):
            cols = half_columns(packed, t, place[0], stat_ref.shape[2])
            stat_ref[t] = jnp.dot(turned[t], cols, preferred_element_type=jnp.float32)

    at = 0
    mine, other = ring_rows(shards, 0, rows), ring_rows(shards, held, rows)
    for d in range(8):
        for ref, start, count in mine[d] + other[d]:
            xs[pl.ds(at, count), :] = ref[pl.ds(start, count), :]
            at += count
    both = turned[...].reshape(-1, turned.shape[2])
    grad = jnp.dot(both, xs[...], preferred_element_type=jnp.float32)
    acc_ref[...] = grad.reshape(acc_ref.shape)

    @pl.when(k == place[2])
    def _():
        gram_ref[...] = gram_here(place, xs, gram_ref.shape[0])


def column_spec(array, block):
    return pl.BlockSpec((array.shape[0], block), lambda k: (0, k))


def first_part(source, place, routed, shards, rows, held, slots_here, block):
    width = shards[0].shape[1]
    tokens = routed.shape[0] * rows
    gram_rows = width // routed.shape[0]
    vmem = pl.BlockSpec(memory_space=pltpu.VMEM)
    smem = pl.BlockSpec(memory_space=pltpu.SMEM)
    flops = 2 * slots_here * block * tokens * (width + block // 2)
    return pl.pallas_call(
        functools.partial(first_kernel, rows, held),
        grid=(width // block,),
        out_shape=(
            jax.ShapeDtypeStruct((slots_here, block, width), jnp.float32),
            jax.ShapeDtypeStruct((slots_here, block, block // 2), jnp.float32),
            jax.ShapeDtypeStruct((gram_rows, block), jnp.float32),
        ),
        in_specs=[smem, smem, vmem] + [column_spec(s, block) for s in shards],
        out_specs=(
            pl.BlockSpec((slots_here, block, block), lambda k: (0, 0, k)),
            pl.BlockSpec((slots_here, block, block // 2), lambda k: (0, 0, 0)),
            pl.BlockSpec((gram_rows, block), lambda k: (0, 0)),
        ),
        scratch_shapes=[
            pltpu.VMEM((slots_here, tokens, block), jnp.bfloat16),
            pltpu.VMEM((slots_here, block, tokens), jnp.bfloat16),
            pltpu.VMEM((tokens, block), jnp.bfloat16),
        ],
        compiler_params=pltpu.CompilerParams(vmem_limit_bytes=VMEM_BYTES),
        cost_estimate=pl.CostEstimate(flops=flops, bytes_accessed=16 * 2**20, transcendentals=0),
    )(source, place, routed, *shards)


def last_kernel(rows, first_late, source, place, used, routed_ref, *refs):
    shards, swapped = refs[:9], refs[9:14]
    acc_ref, stat1_ref, gram1_ref, inv_ref, out_ref, stat_ref, gram_ref, packed, turned, xs, a_mat, scale, left_both = refs[14:]
    k = pl.program_id(0)

    @pl.when(k == 0)
    def _():
        total = jnp.zeros(scale.shape, jnp.float32)
        for n in range(routed_ref.shape[0]):
            total += routed_ref[n, pl.ds(turned.shape[0] * rows, scale.shape[0]), :].astype(jnp.float32)
        scale[...] = 1.0 / total
        pack_routed(rows, source, routed_ref, packed, turned)
        for t in range(turned.shape[0]):
            cols = half_columns(packed, t, place[0], stat_ref.shape[2])
            stat = stat1_ref[t] + jnp.dot(turned[t], cols, preferred_element_type=jnp.float32)
            stat = stat * scale[:1, : stat.shape[1]]
            stat_ref[t] = jnp.where(used[t] > 0, stat, 0.0).astype(stat_ref.dtype)

    zero, one, two, three, four = swapped
    late = four.shape[0]
    partner = [(zero, 0), (one, 0), (two, 0), (three, 0), (four, 0), (three, 1), (two, 1), (one, 1)]
    mine = ring_rows(shards, first_late, rows)
    pieces = ring_rows(shards, first_late + rows, late - rows)
    piece = a_mat.shape[0] // 16
    at = 0
    for d in range(8):
        ref, number = partner[d]
        for part, start, count in mine[d] + [(ref, number * late, rows)]:
            xs[pl.ds(at, count), :] = part[pl.ds(start, count), :]
            at += count
        for n, found in enumerate([pieces[d], [(ref, number * late + rows, piece)]]):
            to = pl.multiple_of(source[2 * d + n] * piece, piece)
            for part, start, count in found:
                a_mat[pl.ds(to, count), :] = part[pl.ds(start, count), :]
                to += count

    slots_here, block, tokens = turned.shape
    both = turned[...].reshape(slots_here * block, tokens)
    grads = jnp.dot(both, xs[...], preferred_element_type=jnp.float32)
    for t in range(slots_here):
        grad = acc_ref[t] + grads[t * block : (t + 1) * block]
        grad = (grad * scale[:1]).astype(jnp.bfloat16)
        left = jnp.dot(inv_ref[t], grad, preferred_element_type=jnp.float32)
        left_both[pl.ds(t * block, block), :] = left.astype(jnp.bfloat16)
    scaled = jnp.dot(left_both[...], a_mat[...], preferred_element_type=jnp.float32)
    for t in range(slots_here):
        part = scaled[t * block : (t + 1) * block]
        out_ref[t] = jnp.where(used[t] > 0, part, 0.0).astype(out_ref.dtype)

    @pl.when(k == place[2])
    def _():
        gram_ref[...] = (gram1_ref[...] + gram_here(place, xs, gram_ref.shape[0])) * scale[:1]


def last_part(source, place, used, routed, shards, swapped, acc, stat1, gram1, inverses, rows, first_late):
    width = acc.shape[2]
    slots_here, block = inverses.shape[:2]
    tokens = routed.shape[0] * rows
    vmem = pl.BlockSpec(memory_space=pltpu.VMEM)
    smem = pl.BlockSpec(memory_space=pltpu.SMEM)
    flops = 2 * slots_here * block * width * (tokens + 2 * block)
    return pl.pallas_call(
        functools.partial(last_kernel, rows, first_late),
        grid=(width // block,),
        out_shape=(
            jax.ShapeDtypeStruct((slots_here, block, width), jnp.bfloat16),
            jax.ShapeDtypeStruct((slots_here, block, block // 2), jnp.bfloat16),
            jax.ShapeDtypeStruct(gram1.shape, jnp.float32),
        ),
        in_specs=[smem, smem, smem, vmem]
        + [column_spec(s, block) for s in list(shards) + list(swapped)]
        + [
            pl.BlockSpec((slots_here, block, block), lambda k: (0, 0, k)), vmem, vmem, vmem,
        ],
        out_specs=(
            pl.BlockSpec((slots_here, block, block), lambda k: (0, 0, k)),
            pl.BlockSpec((slots_here, block, block // 2), lambda k: (0, 0, 0)),
            pl.BlockSpec(gram1.shape, lambda k: (0, 0)),
        ),
        scratch_shapes=[
            pltpu.VMEM((slots_here, tokens, block), jnp.bfloat16),
            pltpu.VMEM((slots_here, block, tokens), jnp.bfloat16),
            pltpu.VMEM((tokens, block), jnp.bfloat16),
            pltpu.VMEM((block, block), jnp.bfloat16),
            pltpu.VMEM((16, block), jnp.float32),
            pltpu.VMEM((slots_here * block, block), jnp.bfloat16),
        ],
        compiler_params=pltpu.CompilerParams(vmem_limit_bytes=VMEM_BYTES),
        cost_estimate=pl.CostEstimate(flops=flops, bytes_accessed=24 * 2**20, transcendentals=0),
    )(source, place, used, routed, *shards, *swapped, acc, stat1, gram1, inverses)


def local(activations, cotangents, mb_count, mb_size, block_slot, inv_blocks):
    rows = activations.shape[2]
    width = activations.shape[3]
    hidden_width = cotangents.shape[3]
    block = inv_blocks.shape[2]
    slots_here = inv_blocks.shape[1]
    half_width = width // 2
    hidden_blocks = hidden_width // block
    input_blocks = half_width // block
    section_count = lax.axis_size("section")
    dp_count = lax.axis_size("dp")
    section_id = lax.axis_index("section")
    dp_id = lax.axis_index("dp")
    half = (section_id >= section_count // 2).astype(jnp.int32)
    zero_bf = jnp.zeros((), jnp.bfloat16)
    mirror = [(s, section_count - 1 - s) for s in range(section_count)]

    x_all = activations[0, 0]
    g_raw = cotangents[0, 0]
    local_blocks = inv_blocks[0]
    meta = jnp.concatenate([mb_count[0], mb_size[0, 0]])
    x_sent = lax.dynamic_slice_in_dim(x_all, (1 - half) * half_width, half_width, 1)

    def limits(numbers):
        return jnp.where(jnp.arange(MB, dtype=jnp.int32) < numbers[0], numbers[1:], 0)

    slot_table = block_slot[0]
    hidden_table = slot_table[:hidden_blocks]
    input_table = slot_table[hidden_blocks:]
    hidden_ids = jnp.arange(hidden_blocks, dtype=jnp.int32)
    every_slot = jnp.arange(dp_count * slots_here, dtype=jnp.int32)
    slot_matches = hidden_table[None, :] == every_slot[:, None]
    block_pick = jnp.sum(jnp.where(slot_matches, hidden_ids[None, :], 0), axis=1)
    my_slots = dp_id * slots_here + jnp.arange(slots_here, dtype=jnp.int32)
    used_here = jnp.any(hidden_table[None, :] == my_slots[:, None], axis=1).astype(jnp.int32)

    live_own = live_mask(meta[0], meta[1:], rows, rows // MB)
    x_own = lax.dynamic_slice_in_dim(x_all, half * half_width, half_width, 1)
    x_own = jnp.where(live_own[:, None], x_own, zero_bf)
    out_own = route(block_pick, limits(meta), jnp.zeros((1,), jnp.int32), g_raw, local_blocks, dp_count, slots_here, block)
    x_far, out_own, meta_sent, x_sent, g_sent = lax.optimization_barrier((x_swap(x_own), out_own, meta, x_sent, g_raw))
    meta_m = lax.ppermute(meta_sent, "section", mirror)
    x_m = lax.ppermute(x_sent, "section", mirror)
    g_m = lax.ppermute(g_sent, "section", mirror)
    live_mir = live_mask(meta_m[0], meta_m[1:], rows, rows // MB)
    count = jnp.sum(live_own.astype(jnp.int32)) + jnp.sum(live_mir.astype(jnp.int32))
    x_mir = jnp.where(live_mir[:, None], x_m, zero_bf)
    own0 = jnp.concatenate([x_own, x_far], axis=0)

    in_own = lax.all_to_all(out_own, "dp", split_axis=0, concat_axis=0, tiled=True)
    own_up1, own_down1 = ring_start(own0)

    piece = block // dp_count
    pieces = in_own[:, slots_here * rows :].reshape(dp_count * slots_here, piece, block)
    mine = jnp.take(pieces, input_table, axis=0).transpose(1, 0, 2).reshape(piece, half_width)
    mir0 = jnp.concatenate([x_mir, mine], axis=0)
    up1, down1 = ring_start(mir0)
    zero = x_swap(mir0)
    own_up2, own_down2 = ring_start_pair(own_up1, own_down1)
    up1, down1, own_up2, own_down2, g_m = lax.optimization_barrier((up1, down1, own_up2, own_down2, g_m))
    one = x_swap(jnp.concatenate([up1, down1], axis=0))
    up2, down2 = ring_start_pair(up1, down1)
    own_up3, own_down3 = ring_start_pair(own_up2, own_down2)
    out_mir = route(block_pick, limits(meta_m), count.reshape(1), g_m, None, dp_count, slots_here, block)
    up2, down2, own_up3, own_down3, out_mir, zero = lax.optimization_barrier((up2, down2, own_up3, own_down3, out_mir, zero))
    two = x_swap(jnp.concatenate([up2, down2], axis=0))
    up3, down3 = ring_start_pair(up2, down2)
    own_top4, own_bottom4 = ring_end(own_up3, own_down3)
    up3, down3, own_top4, own_bottom4, one = lax.optimization_barrier((up3, down3, own_top4, own_bottom4, one))
    three = x_swap(jnp.concatenate([up3, down3], axis=0))
    top4, bottom4 = ring_end(up3, down3)
    top4, bottom4, out_mir, two = lax.optimization_barrier((top4, bottom4, out_mir, two))
    four = x_swap(jnp.concatenate([top4, bottom4], axis=0))
    own_shards = [own0, own_up1, own_up2, own_up3, own_top4, own_bottom4, own_down3, own_down2, own_down1]
    shards = [mir0, up1, up2, up3, top4, bottom4, down3, down2, down1]

    in_mir = lax.all_to_all(out_mir, "dp", split_axis=0, concat_axis=0, tiled=True)

    z_count = dp_count // 2
    z_from = lax.rem(dp_id // 2 - jnp.arange(z_count, dtype=jnp.int32) + z_count, z_count)
    x_here = lax.rem(dp_id, 2)
    x_order = jnp.stack([x_here, 1 - x_here])
    source = (z_from[:, None] * 2 + x_order[None, :]).reshape(-1)
    per_block = dp_count // input_blocks
    place = jnp.stack([half, dp_id, dp_id // per_block, lax.rem(dp_id, per_block)]).astype(jnp.int32)

    swapped = [zero, one, two, three, four]
    acc, stat1, gram1 = first_part(source, place, in_own, own_shards, rows, rows, slots_here, block)
    preconditioned, output_stats, input_stats = last_part(
        source, place, used_here, in_mir, shards, swapped, acc, stat1, gram1, local_blocks,
        rows, 0,
    )
    return (preconditioned[None], output_stats[None], input_stats[None])


def solution(mesh):
    in_specs = (
        P("section", "dp", None, None),
        P("section", "dp", None, None),
        P("section", "dp"),
        P("section", "dp", None),
        P("section", None),
        P("section", "dp", None, None),
    )
    out_specs = (
        P("section", "dp", None, None),
        P("section", "dp", None, None),
        P("section", "dp", None),
    )
    return jax.shard_map(local, mesh=mesh, in_specs=in_specs, out_specs=out_specs, check_vma=False)
```
